32 devices in a mesh: seed: 4 (over x, core), chan: 2 (over y), fsdp: 4 (over z).
Axes of the slice: x: 2, y: 2, z: 4, core: 2. Of those that a mesh axis runs over, the one named last changes fastest.
Arguments:
- stream: bfloat16 [256, 144, 8192], P(('seed', 'fsdp'), None, 'chan'), parts along dimension 0, may hold values from -12.5 to 9.5
- mid: bfloat16 [256, 144, 2048], P(('seed', 'fsdp'), None, 'chan'), parts along dimension 0, may hold values from 0 to 2
- conv_weight: bfloat16 [8192, 8192], P(('seed', 'fsdp'), 'chan'), parts along dimension 0, may hold values from -0.125 to 0.125
- head_weight: bfloat16 [32768, 16384], P(('seed', 'chan'), 'fsdp'), parts along dimension 0, may hold values from -0.375 to 0.375
- labels: int32 [64], replicated, may hold values from 0 to 16383
- proj_act: bfloat16 [2048, 32], replicated, may hold values from -0.125 to 0.125
- proj_err: bfloat16 [8192, 64], P('chan'), may hold values from -6 to 6
Outputs:
- grad_proj: float32 [256, 2048], P(('seed', 'fsdp'), 'chan'), parts along dimension 0
The draws below stay inside these ranges and needn't reach their ends.
There are 4 independent parts, one for each index of `seed`. The reference program is written for one: setup_inputs(seed, part) draws one part's arguments, and reference() takes and returns one part's arrays. A program takes and returns all parts, laid end to end along the dimension named above; an argument that names none is the same for every part. Nothing has to cross between parts.
All inputs are finite; a program needn't handle non-finite values.
Results may differ from the reference program's by a relative error of at most 0.01.
Values may be sent and summed in bfloat16 or wider, within the bound.
A program may use at most 192 MiB of HBM per device.

```python
import jax
import jax.numpy as jnp
from jax import lax

C = 8192
MID = 2048
CLASSES = 16384
POS = 144
KA = 32
KE = 64
IMAGES = 64


def draw_stream(key, part):
    offset_key = jax.random.fold_in(key, 11)
    noise_key = jax.random.fold_in(key, 23)
    offset = -1.5 + 3.0 * jnp.clip(jax.random.normal(offset_key, (IMAGES, 1, C), jnp.float32), -3.0, 3.0)
    noise = 0.5 * jnp.clip(jax.random.normal(noise_key, (IMAGES, POS, C), jnp.float32), -4.0, 4.0)
    return (offset + noise).astype(jnp.bfloat16)


def plant(drawn, stream_key, least, top_value):
    longest = drawn.shape.index(max(drawn.shape))
    spots = []
    for shift in (0, 1):
        where = [jax.random.randint(jax.random.fold_in(stream_key, axis), (), 0, length) for axis, length in enumerate(drawn.shape)]
        where[longest] = (where[longest] + shift) % drawn.shape[longest]
        spots.append(tuple(where))
    return drawn.at[spots[0]].set(least).at[spots[1]].set(top_value)


def block_scale(stream_key, dims, shards, smallest, largest):
    gain, own = 1.0, jax.random.fold_in(stream_key, 6)
    for axis_at, parts in shards:
        steps = jnp.exp(jax.random.uniform(jax.random.fold_in(own, axis_at), (parts,), jnp.float32, smallest / len(shards), largest / len(shards)))
        gain = gain * jnp.repeat(steps, dims[axis_at] // parts).reshape([-1 if axis == axis_at else 1 for axis in range(len(dims))])
    return gain


def bell_draw(rng, dims, spread, most, shards=(), kind=jnp.bfloat16):
    result = spread * jax.random.normal(rng, dims, jnp.float32)
    if shards:
        result = result * block_scale(rng, dims, shards, -0.22, 0.18)
    return jnp.clip(result, -most, most).astype(kind)


def setup_inputs(seed: int = 0, part: int = 0) -> dict:
    key_of = jax.random.split(jax.random.key(seed), 8)
    own_keys = jax.random.split(jax.random.fold_in(key_of[7], part), 8)
    stream = draw_stream(jax.random.fold_in(jax.random.fold_in(key_of[7], part), 71), part)
    mid = jnp.clip(2.0 * jax.random.uniform(own_keys[1], (IMAGES, POS, MID), jnp.float32) ** block_scale(own_keys[1], (IMAGES, POS, MID), ((0, 4), (2, 2)), -0.2, 0.2), 0.0, 2.0).astype(jnp.bfloat16)
    conv_weight = bell_draw(own_keys[2], (MID, C), MID ** -0.5, 0.125, ((0, 4), (1, 2)))
    head_weight = bell_draw(own_keys[3], (C, CLASSES), (C // 32) ** -0.5, 0.375, ((0, 2), (1, 4)))
    labels = plant(jax.random.randint(key_of[4], (IMAGES,), 0, CLASSES), jax.random.fold_in(key_of[4], 1), 0, CLASSES - 1).astype(jnp.int32)
    proj_act = bell_draw(key_of[5], (MID, KA), MID ** -0.5, 0.125)
    proj_err = bell_draw(key_of[6], (C, KE), 1.0, 6.0, ((0, 2),))
    return dict(stream=stream, mid=mid, conv_weight=conv_weight, head_weight=head_weight, labels=labels, proj_act=proj_act, proj_err=proj_err)


def reference(stream, mid, conv_weight, head_weight, labels, proj_act, proj_err):
    images = stream.shape[0]
    mid_rows = mid.reshape(images * POS, MID)
    conv_out = jnp.dot(mid_rows, conv_weight, preferred_element_type=jnp.float32).reshape(images, POS, C)
    y_full = stream.astype(jnp.float32) + conv_out
    pooled = jnp.mean(jnp.maximum(y_full, 0.0), axis=1).astype(jnp.bfloat16)
    logits = jnp.dot(pooled, head_weight, preferred_element_type=jnp.float32)
    expo = jnp.exp(logits)
    total = jnp.sum(expo, axis=1, keepdims=True)
    onehot = (labels[:, None] == jnp.arange(CLASSES, dtype=jnp.int32)[None, :]).astype(jnp.float32)
    dlogits = (expo / total - onehot).astype(jnp.bfloat16)
    dpooled = jnp.dot(dlogits, head_weight.T, preferred_element_type=jnp.float32)
    error = jnp.where(y_full > 0.0, dpooled[:, None, :] / POS, 0.0).astype(jnp.bfloat16)
    acts_proj = jnp.dot(mid_rows, proj_act, preferred_element_type=jnp.float32).reshape(images, POS, KA)
    err_proj = jnp.dot(error.reshape(images * POS, C), proj_err, preferred_element_type=jnp.float32).reshape(images, POS, KE)
    grads = jnp.einsum("npa,npb->nab", acts_proj, err_proj, precision=lax.Precision.HIGHEST)
    return grads.reshape(images, KA * KE)
```

```python
import functools

import jax
import jax.numpy as jnp
from jax import lax
from jax.experimental import pallas as pl
from jax.experimental.pallas import tpu as pltpu
from jax.sharding import PartitionSpec as P

MESH = pl.DeviceIdType.MESH
AHEAD = 3


def conv_kernel(
    nc, nf, positions, group,
    stream_ref, mid_ref, weight_ref, proj_ref,
    pooled_ref, cross_ref,
    weights, mids, acts, held,
    own_sem, right_sem, left_sem, in_sem, mid_send, mid_recv, mid_own, held_sem,
):
    c = lax.axis_index("chan")
    f = lax.axis_index("fsdp")
    chunks, depth, cw = weights.shape[1:]
    share = mids.shape[2]
    rows = mids.shape[1]
    images = rows // positions

    def own_copy(j):
        return pltpu.make_async_copy(
            weight_ref.at[:, pl.ds(pl.multiple_of(j * cw, cw), cw)], weights.at[f, j], own_sem.at[j]
        )

    def hop(b, j, right):
        return pltpu.make_async_remote_copy(
            src_ref=weights.at[b, j],
            dst_ref=weights.at[b, j],
            send_sem=(right_sem if right else left_sem).at[b, j],
            recv_sem=in_sem.at[b, j],
            device_id={"fsdp": f + 1 if right else f - 1},
            device_id_type=MESH,
        )

    def mid_copy(d):
        to = lax.rem(c + d, nc)
        return pltpu.make_async_remote_copy(
            src_ref=mid_ref,
            dst_ref=mids.at[c],
            send_sem=mid_send.at[d],
            recv_sem=mid_recv.at[d],
            device_id={"chan": to},
            device_id_type=MESH,
        )

    def stream_copy(k):
        slot = lax.rem(k, 2)
        return pltpu.make_async_copy(
            stream_ref.at[:, pl.ds(pl.multiple_of(k * cw, cw), cw)], held.at[slot], held_sem.at[slot]
        )

    lax.fori_loop(0, chunks, lambda j, x: (own_copy(j).start(), x)[1], 0)
    own_mid = pltpu.make_async_copy(mid_ref, mids.at[c], mid_own)
    own_mid.start()
    stream_copy(0).start()

    barrier = pltpu.get_barrier_semaphore()
    for d in range(1, nc):
        pl.semaphore_signal(barrier, 1, device_id={"chan": lax.rem(c + d, nc)}, device_id_type=MESH)

    @pl.when(f > 0)
    def _():
        pl.semaphore_signal(barrier, 1, device_id={"fsdp": f - 1}, device_id_type=MESH)

    @pl.when(f < nf - 1)
    def _():
        pl.semaphore_signal(barrier, 1, device_id={"fsdp": f + 1}, device_id_type=MESH)

    ends = jnp.where(f > 0, 1, 0) + jnp.where(f < nf - 1, 1, 0)
    pl.semaphore_wait(barrier, nc - 1 + ends)

    for d in range(1, nc):
        mid_copy(d).start()

    def send_own(j):
        own_copy(j).wait()

        @pl.when(f < nf - 1)
        def _():
            hop(f, j, True).start()

        @pl.when(f > 0)
        def _():
            hop(f, j, False).start()

    for j in range(min(AHEAD, chunks)):
        send_own(j)

    def relay(r):
        @pl.when(r + AHEAD < chunks)
        def _():
            send_own(r + AHEAD)

        for d in range(1, nf):
            @pl.when(f - d >= 0)
            def _():
                hop(f - d, r, True).wait_recv()

                @pl.when(f < nf - 1)
                def _():
                    hop(f - d, r, True).start()

            @pl.when(f + d < nf)
            def _():
                hop(f + d, r, False).wait_recv()

                @pl.when(f > 0)
                def _():
                    hop(f + d, r, False).start()

    step = min(depth, share)
    pieces = nf * depth // step

    def compute(k):
        stream_copy(k).wait()

        @pl.when(k + 1 < chunks)
        def _():
            stream_copy(k + 1).start()

        slot = lax.rem(k, 2)
        columns = pl.ds(pl.multiple_of(k * cw, cw), cw)

        def some(g, x):
            span = pl.ds(pl.multiple_of(g * group * positions, 16), group * positions)
            y = held[slot, span, :].astype(jnp.float32)
            for s in range(pieces):
                at = s * step
                y += jnp.dot(
                    mids[at // share, span, at % share : at % share + step],
                    weights[at // depth, k, at % depth : at % depth + step, :],
                    preferred_element_type=jnp.float32,
                )
            total = []
            for i in range(group):
                one = y[i * positions : (i + 1) * positions]
                total.append(jnp.sum(jnp.maximum(one, 0.0), axis=0, keepdims=True))
                mask = jnp.where(one > 0.0, 1.0, 0.0).astype(jnp.bfloat16)
                cross_ref[g * group + i, :, columns] = jnp.dot(
                    acts[g * group + i], mask, preferred_element_type=jnp.float32
                )
            mean = jnp.concatenate(total, axis=0) / positions
            pooled_ref[g, :, columns] = mean
            return x

        lax.fori_loop(0, images // group, some, 0)

    def project():
        own_mid.wait()
        for d in range(1, nc):
            mid_copy(d).wait_recv()

        def one(i, x):
            span = pl.ds(pl.multiple_of(i * positions, 16), positions)
            out = jnp.zeros((proj_ref.shape[0], positions), jnp.float32)
            for q in range(nc):
                out += lax.dot_general(
                    proj_ref[:, q * share : (q + 1) * share], mids[q, span, :],
                    (((1,), (1,)), ((), ())), preferred_element_type=jnp.float32,
                )
            acts[i] = out.astype(jnp.bfloat16)
            return x

        lax.fori_loop(0, images, one, 0)

    first = max(chunks // 2 - 1, 0)
    last = max(chunks - 2, 0)
    lax.fori_loop(0, first, lambda r, x: (relay(r), x)[1], 0)
    project()

    def pair(r, x):
        relay(r)
        compute(2 * (r - first))
        compute(2 * (r - first) + 1)
        return x

    lax.fori_loop(first, last, pair, 0)

    def single(r, x):
        relay(r)
        compute(r)
        return x

    lax.fori_loop(last, chunks, single, 0)

    def drain(j, x):
        @pl.when(f < nf - 1)
        def _():
            hop(f, j, True).wait_send()

        @pl.when(f > 0)
        def _():
            hop(f, j, False).wait_send()

        for d in range(1, nf):
            @pl.when((f - d >= 0) & (f < nf - 1))
            def _():
                hop(f - d, j, True).wait_send()

            @pl.when((f + d < nf) & (f > 0))
            def _():
                hop(f + d, j, False).wait_send()

        return x

    lax.fori_loop(0, chunks, drain, 0)
    for d in range(1, nc):
        mid_copy(d).wait_send()


def conv(stream, mid, weight, proj_t, nc, nf):
    images, positions, width = stream.shape
    rows = images * positions
    share = mid.shape[2]
    depth = weight.shape[0]
    ka = proj_t.shape[0]
    cw = min(256, width)
    chunks = width // cw
    group = 4
    vmem = pl.BlockSpec(memory_space=pltpu.VMEM)
    hbm = pl.BlockSpec(memory_space=pl.ANY)
    dma = pltpu.SemaphoreType.DMA
    pooled, cross = pl.pallas_call(
        functools.partial(conv_kernel, nc, nf, positions, group),
        out_shape=(
            jax.ShapeDtypeStruct((images // group, group, width), jnp.float32),
            jax.ShapeDtypeStruct((images, ka, width), jnp.float32),
        ),
        in_specs=[hbm, hbm, hbm, vmem],
        out_specs=(vmem, vmem),
        scratch_shapes=[
            pltpu.VMEM((nf, chunks, depth, cw), jnp.bfloat16),
            pltpu.VMEM((nc, rows, share), jnp.bfloat16),
            pltpu.VMEM((images, ka, positions), jnp.bfloat16),
            pltpu.VMEM((2, rows, cw), jnp.bfloat16),
            dma((chunks,)),
            dma((nf, chunks)),
            dma((nf, chunks)),
            dma((nf, chunks)),
            dma((nc,)),
            dma((nc,)),
            dma,
            dma((2,)),
        ],
        compiler_params=pltpu.CompilerParams(
            collective_id=0, has_side_effects=True, vmem_limit_bytes=56 * 2**20
        ),
        cost_estimate=pl.CostEstimate(
            flops=2 * rows * width * depth * nf,
            bytes_accessed=2 * rows * width + 2 * depth * nf * width,
            transcendentals=0,
        ),
    )(stream.reshape(rows, width), mid.reshape(rows, share), weight, proj_t)
    return pooled.reshape(images, width).astype(jnp.bfloat16), cross


def per_device(nc, nf, stream, mid, conv_weight, head_weight, labels, proj_act, proj_err):
    images, positions, width = stream.shape
    pooled, cross = conv(stream, mid, conv_weight, proj_act.T, nc, nf)
    pooled_all = lax.all_gather(pooled, "fsdp", axis=0, tiled=True)
    partial_value = jnp.dot(pooled_all, head_weight, preferred_element_type=jnp.float32)
    block = head_weight.shape[1]
    block_start = lax.axis_index("fsdp") * block
    logits = lax.psum(partial_value, "chan")
    expo = jnp.exp(logits)
    total = lax.psum(jnp.sum(expo, axis=1), "fsdp")
    classes = block_start + jnp.arange(block, dtype=jnp.int32)
    onehot = (labels[:, None] == classes[None, :]).astype(jnp.float32)
    dlogits = (expo / total[:, None] - onehot).astype(jnp.bfloat16)
    dpooled = lax.psum_scatter(
        lax.dot_general(
            dlogits, head_weight, (((1,), (1,)), ((), ())), preferred_element_type=jnp.float32
        ),
        "fsdp",
        scatter_dimension=0,
        tiled=True,
    )
    error = (dpooled / positions).astype(jnp.bfloat16).astype(jnp.float32)
    scaled = (cross * error[:, None, :]).astype(jnp.bfloat16)
    ka = cross.shape[1]
    grads = jnp.dot(
        scaled.reshape(images * ka, width), proj_err, preferred_element_type=jnp.float32
    ).reshape(images, ka * proj_err.shape[1])
    return lax.psum_scatter(grads, "chan", scatter_dimension=1, tiled=True)


def solution(mesh):
    in_specs = (
        P(("seed", "fsdp"), None, "chan"),
        P(("seed", "fsdp"), None, "chan"),
        P(("seed", "fsdp"), "chan"),
        P(("seed", "chan"), "fsdp"),
        P(),
        P(),
        P("chan", None),
    )
    out_specs = P(("seed", "fsdp"), "chan")
    return jax.shard_map(
        functools.partial(per_device, mesh.shape["chan"], mesh.shape["fsdp"]),
        mesh=mesh, in_specs=in_specs, out_specs=out_specs, check_vma=False,
    )
```

```python
import functools

import jax
import jax.numpy as jnp
from jax import lax
from jax.experimental import pallas as pl
from jax.experimental.pallas import tpu as pltpu
from jax.sharding import PartitionSpec as P

MESH = pl.DeviceIdType.MESH
AHEAD = 3


def trak_kernel(
    nc, nf, positions, group,
    stream_ref, mid_ref, weight_ref, proj_ref, head_ref, labels_ref, perr_ref,
    out_ref,
    weights, mids, acts, held, cross, mean, pools, heads, logits, logits_in,
    totals, dlogits, dpool, dpool_in, perr, grads, shares, shares_in,
    own_sem, right_sem, left_sem, in_sem, mid_send, mid_recv, mid_own, held_sem,
    pool_send, pool_recv, head_sem, logit_send, logit_recv, total_send, total_recv,
    dlog_send, dlog_recv, dpool_send, dpool_recv, perr_sem, share_send, share_recv,
):
    c = lax.axis_index("chan")
    f = lax.axis_index("fsdp")
    chunks, depth, cw = weights.shape[1:]
    share = mids.shape[2]
    rows = mids.shape[1]
    images = rows // positions

    def own_copy(j):
        return pltpu.make_async_copy(
            weight_ref.at[:, pl.ds(pl.multiple_of(j * cw, cw), cw)], weights.at[f, j], own_sem.at[j]
        )

    def hop(b, j, right):
        return pltpu.make_async_remote_copy(
            src_ref=weights.at[b, j],
            dst_ref=weights.at[b, j],
            send_sem=(right_sem if right else left_sem).at[b, j],
            recv_sem=in_sem.at[b, j],
            device_id={"fsdp": f + 1 if right else f - 1},
            device_id_type=MESH,
        )

    def mid_copy(d):
        to = lax.rem(c + d, nc)
        return pltpu.make_async_remote_copy(
            src_ref=mid_ref,
            dst_ref=mids.at[c],
            send_sem=mid_send.at[d],
            recv_sem=mid_recv.at[d],
            device_id={"chan": to},
            device_id_type=MESH,
        )

    def stream_copy(k):
        slot = lax.rem(k, 2)
        return pltpu.make_async_copy(
            stream_ref.at[:, pl.ds(pl.multiple_of(k * cw, cw), cw)], held.at[slot], held_sem.at[slot]
        )

    lax.fori_loop(0, chunks, lambda j, x: (own_copy(j).start(), x)[1], 0)
    own_mid = pltpu.make_async_copy(mid_ref, mids.at[c], mid_own)
    own_mid.start()
    stream_copy(0).start()

    classes = head_ref.shape[1]
    tile = min(1024, classes)
    slots = heads.shape[0]
    part = logits.shape[1]

    def head_copy(t):
        slot = lax.rem(t, slots)
        return pltpu.make_async_copy(
            head_ref.at[pl.ds(pl.multiple_of(lax.rem(t, chunks) * cw, cw), cw), :],
            heads.at[slot], head_sem.at[slot],
        )

    def to_chan(src, dst, send, recv, d):
        return pltpu.make_async_remote_copy(
            src_ref=src, dst_ref=dst, send_sem=send.at[d], recv_sem=recv.at[d],
            device_id={"chan": lax.rem(c + d, nc)}, device_id_type=MESH,
        )

    def to_fsdp(src, dst, send, recv, d):
        return pltpu.make_async_remote_copy(
            src_ref=src, dst_ref=dst, send_sem=send, recv_sem=recv,
            device_id={"fsdp": lax.rem(f + d, nf)}, device_id_type=MESH,
        )

    def pool_copy(k, d):
        return to_fsdp(pools.at[k, f], pools.at[k, f], pool_send.at[d, k], pool_recv.at[d, k], d)

    def logit_copy(d):
        return to_chan(logits.at[lax.rem(c + d, nc)], logits_in.at[c], logit_send, logit_recv, d)

    def total_copy(d):
        return to_fsdp(totals.at[f], totals.at[f], total_send.at[d], total_recv.at[d], d)

    def dlog_copy(d):
        return to_chan(dlogits.at[c], dlogits.at[c], dlog_send, dlog_recv, d)

    def dpool_copy(k, d):
        return to_fsdp(
            dpool.at[k, lax.rem(f + d, nf)], dpool_in.at[k, f], dpool_send.at[d, k], dpool_recv.at[d, k], d
        )

    def share_copy(d):
        return to_chan(shares.at[lax.rem(c + d, nc)], shares_in.at[c], share_send, share_recv, d)

    for t in range(slots):
        head_copy(t).start()
    perr_copy = pltpu.make_async_copy(perr_ref, perr.at[0 : perr_ref.shape[0]], perr_sem)
    perr_copy.start()
    perr[perr_ref.shape[0] :] = jnp.zeros(
        (perr.shape[0] - perr_ref.shape[0], perr.shape[1]), perr.dtype
    )
    logits[...] = jnp.zeros_like(logits)

    barrier = pltpu.get_barrier_semaphore()
    for d in range(1, nc):
        pl.semaphore_signal(barrier, 1, device_id={"chan": lax.rem(c + d, nc)}, device_id_type=MESH)

    for d in range(1, nf):
        pl.semaphore_signal(barrier, 1, device_id={"fsdp": lax.rem(f + d, nf)}, device_id_type=MESH)
    pl.semaphore_wait(barrier, nc - 1 + nf - 1)

    for d in range(1, nc):
        mid_copy(d).start()

    def send_own(j):
        own_copy(j).wait()

        @pl.when(f < nf - 1)
        def _():
            hop(f, j, True).start()

        @pl.when(f > 0)
        def _():
            hop(f, j, False).start()

    for j in range(min(AHEAD, chunks)):
        send_own(j)

    def relay(r):
        @pl.when(r + AHEAD < chunks)
        def _():
            send_own(r + AHEAD)

        for d in range(1, nf):
            @pl.when(f - d >= 0)
            def _():
                hop(f - d, r, True).wait_recv()

                @pl.when(f < nf - 1)
                def _():
                    hop(f - d, r, True).start()

            @pl.when(f + d < nf)
            def _():
                hop(f + d, r, False).wait_recv()

                @pl.when(f > 0)
                def _():
                    hop(f + d, r, False).start()

    step = min(depth, share)
    pieces = nf * depth // step

    def compute(k):
        stream_copy(k).wait()

        @pl.when(k + 1 < chunks)
        def _():
            stream_copy(k + 1).start()

        slot = lax.rem(k, 2)

        def some(g, x):
            span = pl.ds(pl.multiple_of(g * group * positions, 16), group * positions)
            y = held[slot, span, :].astype(jnp.float32)
            for s in range(pieces):
                at = s * step
                y += jnp.dot(
                    mids[at // share, span, at % share : at % share + step],
                    weights[at // depth, k, at % depth : at % depth + step, :],
                    preferred_element_type=jnp.float32,
                )
            for i in range(group):
                one = y[i * positions : (i + 1) * positions]
                total = jnp.sum(jnp.maximum(one, 0.0), axis=0, keepdims=True)
                mean[pl.ds(g * group + i, 1), :] = total / positions
                mask = jnp.where(one > 0.0, 1.0, 0.0).astype(jnp.bfloat16)
                cross[k, g * group + i] = jnp.dot(
                    acts[g * group + i], mask, preferred_element_type=jnp.float32
                ).astype(cross.dtype)
            return x

        lax.fori_loop(0, images // group, some, 0)
        pools[k, f] = mean[...].astype(jnp.bfloat16)
        for d in range(1, nf):
            pool_copy(k, d).start()

    def add_logits(k):
        head_copy(k).wait()
        for d in range(1, nf):
            pool_copy(k, d).wait_recv()
        slot = lax.rem(k, slots)
        rows_all = pools[k].reshape(nf * images, cw)

        def some(g, x):
            span = pl.ds(pl.multiple_of(g * tile, tile), tile)
            add = jnp.dot(rows_all, heads[slot, :, span], preferred_element_type=jnp.float32)
            for q in range(nc):
                logits[q, :, span] += add[q * part : (q + 1) * part]
            return x

        lax.fori_loop(0, classes // tile, some, 0)
        head_copy(k + slots).start()

    def project():
        own_mid.wait()
        for d in range(1, nc):
            mid_copy(d).wait_recv()

        def one(i, x):
            span = pl.ds(pl.multiple_of(i * positions, 16), positions)
            out = jnp.zeros((proj_ref.shape[0], positions), jnp.float32)
            for q in range(nc):
                out += lax.dot_general(
                    proj_ref[:, q * share : (q + 1) * share], mids[q, span, :],
                    (((1,), (1,)), ((), ())), preferred_element_type=jnp.float32,
                )
            acts[i] = out.astype(jnp.bfloat16)
            return x

        lax.fori_loop(0, images, one, 0)

    first = max(chunks // 2 - 1, 0)
    last = max(chunks - 2, 0)
    lax.fori_loop(0, first, lambda r, x: (relay(r), x)[1], 0)
    project()

    def pair(r, x):
        relay(r)
        compute(2 * (r - first))
        compute(2 * (r - first) + 1)

        @pl.when(r > first)
        def _():
            add_logits(2 * (r - first) - 2)
            add_logits(2 * (r - first) - 1)

        return x

    lax.fori_loop(first, last, pair, 0)

    def single(r, x):
        relay(r)
        compute(r)

        @pl.when(r >= 2)
        def _():
            add_logits(r - 2)

        return x

    lax.fori_loop(last, chunks, single, 0)
    for k in range(last, chunks):
        add_logits(k)

    for d in range(1, nc):
        logit_copy(d).start()
    for d in range(1, nc):
        logit_copy(d).wait_recv()

    def exponents(g, total):
        span = pl.ds(pl.multiple_of(g * tile, tile), tile)
        value = logits[c, :, span]
        for d in range(1, nc):
            value += logits_in[lax.rem(c + nc - d, nc), :, span]
        value = jnp.exp(value)
        logits[c, :, span] = value
        return total + jnp.sum(value, axis=1, keepdims=True)

    total = lax.fori_loop(0, classes // tile, exponents, jnp.zeros((part, 1), jnp.float32))
    totals[f] = jnp.broadcast_to(total, totals.shape[1:])
    for d in range(1, nf):
        total_copy(d).start()
    for d in range(1, nf):
        total_copy(d).wait_recv()
    total = jnp.sum(totals[...], axis=0)[:, :1]

    def derivatives(g, x):
        span = pl.ds(pl.multiple_of(g * tile, tile), tile)
        ids = f * classes + g * tile + lax.broadcasted_iota(jnp.int32, (part, tile), 1)
        onehot = jnp.where(labels_ref[c] == ids, 1.0, 0.0)
        dlogits[c, :, span] = (logits[c, :, span] / total - onehot).astype(dlogits.dtype)
        return x

    lax.fori_loop(0, classes // tile, derivatives, 0)
    for d in range(1, nc):
        dlog_copy(d).start()
    for d in range(1, nc):
        dlog_copy(d).wait_recv()

    def back(k, x):
        head_copy(k + chunks).wait()
        slot = lax.rem(k + chunks, slots)
        grad = lax.dot_general(
            dlogits[...].reshape(nc * part, classes).astype(jnp.bfloat16), heads[slot],
            (((1,), (1,)), ((), ())), preferred_element_type=jnp.float32,
        )
        dpool[k] = grad.reshape(nf, images, cw).astype(jnp.bfloat16)
        for d in range(1, nf):
            dpool_copy(k, d).start()

        @pl.when(k + slots < chunks)
        def _():
            head_copy(k + chunks + slots).start()

        return x

    lax.fori_loop(0, chunks, back, 0)
    perr_copy.wait()
    grads[...] = jnp.zeros_like(grads)

    def finish(k, x):
        error = dpool[k, f].astype(jnp.float32)
        for d in range(1, nf):
            dpool_copy(k, d).wait_recv()
        for d in range(1, nf):
            error += dpool_in[k, lax.rem(f + nf - d, nf)].astype(jnp.float32)
        error = (error / positions).astype(jnp.bfloat16).astype(jnp.float32)
        scaled = jnp.concatenate(
            [
                (cross[k, i].astype(jnp.float32) * error[i : i + 1]).astype(jnp.bfloat16)
                for i in range(images)
            ],
            axis=0,
        )
        grads[...] += lax.dot_general(
            scaled, perr[:, pl.ds(pl.multiple_of(k * cw, cw), cw)],
            (((1,), (1,)), ((), ())), preferred_element_type=jnp.float32,
        )
        return x

    lax.fori_loop(0, chunks, finish, 0)
    ka = proj_ref.shape[0]
    kq = ka // nc
    for q in range(nc):
        for i in range(images):
            shares[q, i] = grads[i * ka + q * kq : i * ka + (q + 1) * kq]
    for d in range(1, nc):
        share_copy(d).start()
    for d in range(1, nc):
        share_copy(d).wait_recv()
    result = shares[c]
    for d in range(1, nc):
        result += shares_in[lax.rem(c + nc - d, nc)]
    out_ref[...] = result

    def drain(j, x):
        @pl.when(f < nf - 1)
        def _():
            hop(f, j, True).wait_send()

        @pl.when(f > 0)
        def _():
            hop(f, j, False).wait_send()

        for d in range(1, nf):
            pool_copy(j, d).wait_send()
            dpool_copy(j, d).wait_send()

            @pl.when((f - d >= 0) & (f < nf - 1))
            def _():
                hop(f - d, j, True).wait_send()

            @pl.when((f + d < nf) & (f > 0))
            def _():
                hop(f + d, j, False).wait_send()

        return x

    lax.fori_loop(0, chunks, drain, 0)
    for d in range(1, nc):
        mid_copy(d).wait_send()
        logit_copy(d).wait_send()
        dlog_copy(d).wait_send()
        share_copy(d).wait_send()
    for d in range(1, nf):
        total_copy(d).wait_send()


def per_device(nc, nf, stream, mid, conv_weight, head_weight, labels, proj_act, proj_err):
    images, positions, width = stream.shape
    rows = images * positions
    share = mid.shape[2]
    depth = conv_weight.shape[0]
    ka, ke = proj_act.shape[1], proj_err.shape[1]
    classes = head_weight.shape[1]
    everyone = images * nf
    part = everyone // nc
    kq = ka // nc
    lanes = max(ke, 128)
    cw = min(256, width)
    chunks = width // cw
    slots = min(8, chunks)
    group = 4
    vmem = pl.BlockSpec(memory_space=pltpu.VMEM)
    hbm = pl.BlockSpec(memory_space=pl.ANY)
    dma = pltpu.SemaphoreType.DMA
    bf16, f32 = jnp.bfloat16, jnp.float32
    out = pl.pallas_call(
        functools.partial(trak_kernel, nc, nf, positions, group),
        out_shape=jax.ShapeDtypeStruct((images, kq, lanes), f32),
        in_specs=[hbm, hbm, hbm, vmem, hbm, vmem, hbm],
        out_specs=vmem,
        scratch_shapes=[
            pltpu.VMEM((nf, chunks, depth, cw), bf16),
            pltpu.VMEM((nc, rows, share), bf16),
            pltpu.VMEM((images, ka, positions), bf16),
            pltpu.VMEM((2, rows, cw), bf16),
            pltpu.VMEM((chunks, images, ka, cw), bf16),
            pltpu.VMEM((images, cw), f32),
            pltpu.VMEM((chunks, nf, images, cw), bf16),
            pltpu.VMEM((slots, cw, classes), bf16),
            pltpu.VMEM((nc, part, classes), f32),
            pltpu.VMEM((nc, part, classes), f32),
            pltpu.VMEM((nf, part, 128), f32),
            pltpu.VMEM((nc, part, classes), bf16 if part % 16 == 0 else f32),
            pltpu.VMEM((chunks, nf, images, cw), bf16),
            pltpu.VMEM((chunks, nf, images, cw), bf16),
            pltpu.VMEM((lanes, width), bf16),
            pltpu.VMEM((images * ka, lanes), f32),
            pltpu.VMEM((nc, images, kq, lanes), f32),
            pltpu.VMEM((nc, images, kq, lanes), f32),
            dma((chunks,)),
            dma((nf, chunks)),
            dma((nf, chunks)),
            dma((nf, chunks)),
            dma((nc,)),
            dma((nc,)),
            dma,
            dma((2,)),
            dma((nf, chunks)),
            dma((nf, chunks)),
            dma((slots,)),
            dma((nc,)),
            dma((nc,)),
            dma((nf,)),
            dma((nf,)),
            dma((nc,)),
            dma((nc,)),
            dma((nf, chunks)),
            dma((nf, chunks)),
            dma,
            dma((nc,)),
            dma((nc,)),
        ],
        compiler_params=pltpu.CompilerParams(
            collective_id=0, has_side_effects=True, vmem_limit_bytes=62 * 2**20
        ),
        cost_estimate=pl.CostEstimate(
            flops=2 * rows * width * depth * nf + 4 * everyone * width * classes,
            bytes_accessed=2 * rows * width + 2 * depth * width + 4 * width * classes,
            transcendentals=part * classes,
        ),
    )(
        stream.reshape(rows, width), mid.reshape(rows, share), conv_weight, proj_act.T,
        head_weight, labels.reshape(nc, part, 1), proj_err.T,
    )
    return out[:, :, :ke].reshape(images, kq * ke)


def solution(mesh):
    in_specs = (
        P(("seed", "fsdp"), None, "chan"),
        P(("seed", "fsdp"), None, "chan"),
        P(("seed", "fsdp"), "chan"),
        P(("seed", "chan"), "fsdp"),
        P(),
        P(),
        P("chan", None),
    )
    out_specs = P(("seed", "fsdp"), "chan")
    return jax.shard_map(
        functools.partial(per_device, mesh.shape["chan"], mesh.shape["fsdp"]),
        mesh=mesh, in_specs=in_specs, out_specs=out_specs, check_vma=False,
    )
```

```python
import functools

import jax
import jax.numpy as jnp
from jax import lax
from jax.experimental import pallas as pl
from jax.experimental.pallas import tpu as pltpu
from jax.sharding import PartitionSpec as P

MESH = pl.DeviceIdType.MESH
AHEAD = 3


def trak_kernel(
    nc, nf, positions, group, handed,
    stream_ref, mid_ref, weight_ref, proj_ref, head_ref, labels_ref, perr_ref,
    out_ref,
    weights, mids, acts, held, cross, mean, pools, heads, logits, logits_in,
    totals, dlogits, dpool, dpool_in, perr, grads, shares, shares_in,
    own_sem, right_sem, left_sem, in_sem, mid_send, mid_recv, mid_own, held_sem,
    pool_send, pool_recv, head_sem, logit_send, logit_recv, total_send, total_recv,
    dlog_send, dlog_recv, dpool_send, dpool_recv, perr_sem, share_send, share_recv,
    *handed_refs,
):
    c = lax.axis_index("chan")
    f = lax.axis_index("fsdp")
    chunks, depth, cw = weights.shape[1:]
    share = mids.shape[2]
    rows = mids.shape[1]
    images = rows // positions
    full = chunks - handed
    inner = (f > 0) & (f < nf - 1)
    if handed:
        (
            mids_end, streams_end, acts_end, cross_end, piece_send, piece_recv, strip_send, strip_recv,
            pass_send, pass_recv, pool_end_send, cross_end_send, cross_end_recv,
        ) = handed_refs
        inward = jnp.where(f == 0, 1, nf - 2)
        end = jnp.where(f == 1, 0, nf - 1)

    def served(to, j):
        return ((to > 0) & (to < nf - 1)) | (j < full)

    def piece_rows(j):
        return pl.ds(pl.multiple_of(j * positions, 16), positions)

    def piece_copy(j):
        return pltpu.make_async_remote_copy(
            src_ref=mid_ref.at[piece_rows(j)], dst_ref=mids_end.at[c, piece_rows(j)],
            send_sem=piece_send.at[j], recv_sem=piece_recv.at[j],
            device_id={"fsdp": inward}, device_id_type=MESH,
        )

    def strip_copy(j):
        return pltpu.make_async_remote_copy(
            src_ref=stream_ref.at[piece_rows(j), full * cw :], dst_ref=streams_end.at[piece_rows(j)],
            send_sem=strip_send.at[j], recv_sem=strip_recv.at[j],
            device_id={"fsdp": inward}, device_id_type=MESH,
        )

    def pass_copy(j, d):
        return pltpu.make_async_remote_copy(
            src_ref=mids_end.at[c, piece_rows(j)], dst_ref=mids_end.at[c, piece_rows(j)],
            send_sem=pass_send.at[d, j], recv_sem=pass_recv.at[d, j],
            device_id={"chan": lax.rem(c + d, nc)}, device_id_type=MESH,
        )

    def cross_copy(k):
        return pltpu.make_async_remote_copy(
            src_ref=cross_end.at[k - full], dst_ref=cross.at[k],
            send_sem=cross_end_send.at[k - full], recv_sem=cross_end_recv.at[k - full],
            device_id={"fsdp": end}, device_id_type=MESH,
        )

    def own_copy(j):
        return pltpu.make_async_copy(
            weight_ref.at[:, pl.ds(pl.multiple_of(j * cw, cw), cw)], weights.at[f, j], own_sem.at[j]
        )

    def hop(b, j, right):
        return pltpu.make_async_remote_copy(
            src_ref=weights.at[b, j],
            dst_ref=weights.at[b, j],
            send_sem=(right_sem if right else left_sem).at[b, j],
            recv_sem=in_sem.at[b, j],
            device_id={"fsdp": f + 1 if right else f - 1},
            device_id_type=MESH,
        )

    def mid_copy(d):
        to = lax.rem(c + d, nc)
        return pltpu.make_async_remote_copy(
            src_ref=mid_ref,
            dst_ref=mids.at[c],
            send_sem=mid_send.at[d],
            recv_sem=mid_recv.at[d],
            device_id={"chan": to},
            device_id_type=MESH,
        )

    def stream_copy(k):
        slot = lax.rem(k, 2)
        return pltpu.make_async_copy(
            stream_ref.at[:, pl.ds(pl.multiple_of(k * cw, cw), cw)], held.at[slot], held_sem.at[slot]
        )

    lax.fori_loop(0, chunks, lambda j, x: (own_copy(j).start(), x)[1], 0)
    own_mid = pltpu.make_async_copy(mid_ref, mids.at[c], mid_own)
    own_mid.start()
    stream_copy(0).start()

    classes = head_ref.shape[1]
    tile = min(1024, classes)
    slots = heads.shape[0]
    part = logits.shape[1]

    def head_copy(t):
        slot = lax.rem(t, slots)
        return pltpu.make_async_copy(
            head_ref.at[pl.ds(pl.multiple_of(lax.rem(t, chunks) * cw, cw), cw), :],
            heads.at[slot], head_sem.at[slot],
        )

    def to_chan(src, dst, send, recv, d):
        return pltpu.make_async_remote_copy(
            src_ref=src, dst_ref=dst, send_sem=send.at[d], recv_sem=recv.at[d],
            device_id={"chan": lax.rem(c + d, nc)}, device_id_type=MESH,
        )

    def to_fsdp(src, dst, send, recv, d):
        return pltpu.make_async_remote_copy(
            src_ref=src, dst_ref=dst, send_sem=send, recv_sem=recv,
            device_id={"fsdp": lax.rem(f + d, nf)}, device_id_type=MESH,
        )

    def pool_copy(k, d):
        return to_fsdp(pools.at[k, f], pools.at[k, f], pool_send.at[d, k], pool_recv.at[f, k], d)

    def pool_end_copy(k, d):
        return to_fsdp(
            pools.at[k, end], pools.at[k, end], pool_end_send.at[d, k - full], pool_recv.at[end, k], d
        )

    def pool_arrival(k, b):
        return to_fsdp(pools.at[k, b], pools.at[k, b], pool_send.at[1, k], pool_recv.at[b, k], 1)

    def logit_copy(d):
        return to_chan(logits.at[lax.rem(c + d, nc)], logits_in.at[c], logit_send, logit_recv, d)

    def total_copy(d):
        return to_fsdp(totals.at[f], totals.at[f], total_send.at[d], total_recv.at[d], d)

    def dlog_copy(d):
        return to_chan(dlogits.at[c], dlogits.at[c], dlog_send, dlog_recv, d)

    def dpool_copy(k, d):
        return to_fsdp(
            dpool.at[k, lax.rem(f + d, nf)], dpool_in.at[k, f], dpool_send.at[d, k], dpool_recv.at[d, k], d
        )

    def share_copy(d):
        return to_chan(shares.at[lax.rem(c + d, nc)], shares_in.at[c], share_send, share_recv, d)

    for t in range(slots):
        head_copy(t).start()
    perr_copy = pltpu.make_async_copy(perr_ref, perr.at[0 : perr_ref.shape[0]], perr_sem)
    perr_copy.start()
    perr[perr_ref.shape[0] :] = jnp.zeros(
        (perr.shape[0] - perr_ref.shape[0], perr.shape[1]), perr.dtype
    )
    logits[...] = jnp.zeros_like(logits)

    barrier = pltpu.get_barrier_semaphore()
    for d in range(1, nc):
        pl.semaphore_signal(barrier, 1, device_id={"chan": lax.rem(c + d, nc)}, device_id_type=MESH)

    for d in range(1, nf):
        pl.semaphore_signal(barrier, 1, device_id={"fsdp": lax.rem(f + d, nf)}, device_id_type=MESH)
    pl.semaphore_wait(barrier, nc - 1 + nf - 1)

    for d in range(1, nc):
        mid_copy(d).start()

    def send_own(j):
        own_copy(j).wait()

        @pl.when((f < nf - 1) & served(f + 1, j))
        def _():
            hop(f, j, True).start()

        @pl.when((f > 0) & served(f - 1, j))
        def _():
            hop(f, j, False).start()

        if handed:
            @pl.when(jnp.logical_not(inner))
            def _():
                piece_copy(j).start()
                strip_copy(j).start()

    for j in range(min(AHEAD, chunks)):
        send_own(j)

    def relay(r):
        @pl.when(r + AHEAD < chunks)
        def _():
            send_own(r + AHEAD)

        for d in range(1, nf):
            @pl.when((f - d >= 0) & served(f, r))
            def _():
                hop(f - d, r, True).wait_recv()

                @pl.when((f < nf - 1) & served(f + 1, r))
                def _():
                    hop(f - d, r, True).start()

            @pl.when((f + d < nf) & served(f, r))
            def _():
                hop(f + d, r, False).wait_recv()

                @pl.when((f > 0) & served(f - 1, r))
                def _():
                    hop(f + d, r, False).start()

        if handed:
            @pl.when(inner & (r >= chunks // 2))
            def _():
                for q in range(2):
                    j = 2 * (r - chunks // 2) + q
                    piece_copy(j).wait_recv()
                    for d in range(1, nc):
                        pass_copy(j, d).start()

    step = min(depth, share)
    pieces = nf * depth // step

    def compute(k):
        stream_copy(k).wait()

        @pl.when((k + 1 < chunks) & served(f, k + 1))
        def _():
            stream_copy(k + 1).start()

        slot = lax.rem(k, 2)
        convolve(k, mids, acts, lambda span: held[slot, span, :], cross.at[k])
        pools[k, f] = mean[...].astype(jnp.bfloat16)
        for d in range(1, nf):
            pool_copy(k, d).start()

    def compute_end(k):
        at = (k - full) * cw
        convolve(k, mids_end, acts_end, lambda span: streams_end[span, at : at + cw], cross_end.at[k - full])
        pools[k, end] = mean[...].astype(jnp.bfloat16)
        for d in range(1, nf):
            pool_end_copy(k, d).start()
        cross_copy(k).start()

    def convolve(k, mids, acts, load, sums):
        def some(g, x):
            span = pl.ds(pl.multiple_of(g * group * positions, 16), group * positions)
            y = load(span).astype(jnp.float32)
            for s in range(pieces):
                at = s * step
                y += jnp.dot(
                    mids[at // share, span, at % share : at % share + step],
                    weights[at // depth, k, at % depth : at % depth + step, :],
                    preferred_element_type=jnp.float32,
                )
            for i in range(group):
                one = y[i * positions : (i + 1) * positions]
                total = jnp.sum(jnp.maximum(one, 0.0), axis=0, keepdims=True)
                mean[pl.ds(g * group + i, 1), :] = total / positions
                mask = jnp.where(one > 0.0, 1.0, 0.0).astype(jnp.bfloat16)
                sums[g * group + i] = jnp.dot(
                    acts[g * group + i], mask, preferred_element_type=jnp.float32
                ).astype(sums.dtype)
            return x

        lax.fori_loop(0, images // group, some, 0)

    def add_logits(k, late=False):
        head_copy(k).wait()
        for b in range(nf):
            here = f == b
            if late:
                here = inner & (here | (end == b))

            @pl.when(jnp.logical_not(here))
            def _():
                pool_arrival(k, b).wait_recv()

        slot = lax.rem(k, slots)
        rows_all = pools[k].reshape(nf * images, cw)

        def some(g, x):
            span = pl.ds(pl.multiple_of(g * tile, tile), tile)
            add = jnp.dot(rows_all, heads[slot, :, span], preferred_element_type=jnp.float32)
            for q in range(nc):
                logits[q, :, span] += add[q * part : (q + 1) * part]
            return x

        lax.fori_loop(0, classes // tile, some, 0)
        head_copy(k + slots).start()

    def project(mids, acts):
        def one(i, x):
            span = pl.ds(pl.multiple_of(i * positions, 16), positions)
            out = jnp.zeros((proj_ref.shape[0], positions), jnp.float32)
            for q in range(nc):
                out += lax.dot_general(
                    proj_ref[:, q * share : (q + 1) * share], mids[q, span, :],
                    (((1,), (1,)), ((), ())), preferred_element_type=jnp.float32,
                )
            acts[i] = out.astype(jnp.bfloat16)
            return x

        lax.fori_loop(0, images, one, 0)

    first = max(full // 2 - 1, 0)
    last = max(full - 2, 0)
    lax.fori_loop(0, first, lambda r, x: (relay(r), x)[1], 0)
    own_mid.wait()
    for d in range(1, nc):
        mid_copy(d).wait_recv()
    project(mids, acts)

    def pair(r, x):
        relay(r)
        compute(2 * (r - first))
        compute(2 * (r - first) + 1)

        @pl.when(r > first)
        def _():
            add_logits(2 * (r - first) - 2)
            add_logits(2 * (r - first) - 1)

        return x

    lax.fori_loop(first, last, pair, 0)

    def single(r, x):
        relay(r)
        compute(r)

        @pl.when(r >= 2)
        def _():
            add_logits(r - 2)

        return x

    lax.fori_loop(last, full, single, 0)
    if handed:
        @pl.when(inner)
        def _():
            for r in range(full, chunks):
                relay(r)
                compute(r)

            def arrived(j, x):
                strip_copy(j).wait_recv()
                for d in range(1, nc):
                    pass_copy(j, d).wait_recv()
                return x

            lax.fori_loop(0, images, arrived, 0)
            project(mids_end, acts_end)
            for k in range(full, chunks):
                compute_end(k)

    for k in range(last, chunks):
        add_logits(k, k >= full)

    for d in range(1, nc):
        logit_copy(d).start()
    for d in range(1, nc):
        logit_copy(d).wait_recv()

    def exponents(g, total):
        span = pl.ds(pl.multiple_of(g * tile, tile), tile)
        value = logits[c, :, span]
        for d in range(1, nc):
            value += logits_in[lax.rem(c + nc - d, nc), :, span]
        value = jnp.exp(value)
        logits[c, :, span] = value
        return total + jnp.sum(value, axis=1, keepdims=True)

    total = lax.fori_loop(0, classes // tile, exponents, jnp.zeros((part, 1), jnp.float32))
    totals[f] = jnp.broadcast_to(total, totals.shape[1:])
    for d in range(1, nf):
        total_copy(d).start()
    for d in range(1, nf):
        total_copy(d).wait_recv()
    total = jnp.sum(totals[...], axis=0)[:, :1]

    def derivatives(g, x):
        span = pl.ds(pl.multiple_of(g * tile, tile), tile)
        ids = f * classes + g * tile + lax.broadcasted_iota(jnp.int32, (part, tile), 1)
        onehot = jnp.where(labels_ref[c] == ids, 1.0, 0.0)
        dlogits[c, :, span] = (logits[c, :, span] / total - onehot).astype(dlogits.dtype)
        return x

    lax.fori_loop(0, classes // tile, derivatives, 0)
    for d in range(1, nc):
        dlog_copy(d).start()
    for d in range(1, nc):
        dlog_copy(d).wait_recv()

    def back(k, x):
        head_copy(k + chunks).wait()
        slot = lax.rem(k + chunks, slots)
        grad = lax.dot_general(
            dlogits[...].reshape(nc * part, classes).astype(jnp.bfloat16), heads[slot],
            (((1,), (1,)), ((), ())), preferred_element_type=jnp.float32,
        )
        dpool[k] = grad.reshape(nf, images, cw).astype(jnp.bfloat16)
        for d in range(1, nf):
            dpool_copy(k, d).start()

        @pl.when(k + slots < chunks)
        def _():
            head_copy(k + chunks + slots).start()

        return x

    lax.fori_loop(0, chunks, back, 0)
    if handed:
        @pl.when(jnp.logical_not(inner))
        def _():
            for k in range(full, chunks):
                cross_copy(k).wait_recv()

    perr_copy.wait()
    grads[...] = jnp.zeros_like(grads)

    def finish(k, x):
        error = dpool[k, f].astype(jnp.float32)
        for d in range(1, nf):
            dpool_copy(k, d).wait_recv()
        for d in range(1, nf):
            error += dpool_in[k, lax.rem(f + nf - d, nf)].astype(jnp.float32)
        error = (error / positions).astype(jnp.bfloat16).astype(jnp.float32)
        scaled = jnp.concatenate(
            [
                (cross[k, i].astype(jnp.float32) * error[i : i + 1]).astype(jnp.bfloat16)
                for i in range(images)
            ],
            axis=0,
        )
        grads[...] += lax.dot_general(
            scaled, perr[:, pl.ds(pl.multiple_of(k * cw, cw), cw)],
            (((1,), (1,)), ((), ())), preferred_element_type=jnp.float32,
        )
        return x

    lax.fori_loop(0, chunks, finish, 0)
    ka = proj_ref.shape[0]
    kq = ka // nc
    for q in range(nc):
        for i in range(images):
            shares[q, i] = grads[i * ka + q * kq : i * ka + (q + 1) * kq]
    for d in range(1, nc):
        share_copy(d).start()
    for d in range(1, nc):
        share_copy(d).wait_recv()
    result = shares[c]
    for d in range(1, nc):
        result += shares_in[lax.rem(c + nc - d, nc)]
    out_ref[...] = result

    def drain(j, x):
        @pl.when((f < nf - 1) & served(f + 1, j))
        def _():
            for d in range(nf):
                @pl.when(f - d >= 0)
                def _():
                    hop(f - d, j, True).wait_send()

        @pl.when((f > 0) & served(f - 1, j))
        def _():
            for d in range(nf):
                @pl.when(f + d < nf)
                def _():
                    hop(f + d, j, False).wait_send()

        for d in range(1, nf):
            dpool_copy(j, d).wait_send()

            @pl.when(served(f, j))
            def _():
                pool_copy(j, d).wait_send()

        if handed:
            @pl.when(jnp.logical_not(inner))
            def _():
                piece_copy(j).wait_send()
                strip_copy(j).wait_send()

            @pl.when(inner)
            def _():
                for d in range(1, nc):
                    pass_copy(j, d).wait_send()

        return x

    if handed:
        @pl.when(inner)
        def _():
            for k in range(full, chunks):
                cross_copy(k).wait_send()
                for d in range(1, nf):
                    pool_end_copy(k, d).wait_send()

    lax.fori_loop(0, chunks, drain, 0)
    for d in range(1, nc):
        mid_copy(d).wait_send()
        logit_copy(d).wait_send()
        dlog_copy(d).wait_send()
        share_copy(d).wait_send()
    for d in range(1, nf):
        total_copy(d).wait_send()


def per_device(nc, nf, stream, mid, conv_weight, head_weight, labels, proj_act, proj_err):
    images, positions, width = stream.shape
    rows = images * positions
    share = mid.shape[2]
    depth = conv_weight.shape[0]
    ka, ke = proj_act.shape[1], proj_err.shape[1]
    classes = head_weight.shape[1]
    everyone = images * nf
    part = everyone // nc
    kq = ka // nc
    lanes = max(ke, 128)
    cw = min(256, width)
    chunks = width // cw
    slots = min(4, chunks)
    handed = 2 if nf == 4 and chunks == images and chunks >= 16 else 0
    group = 4
    vmem = pl.BlockSpec(memory_space=pltpu.VMEM)
    hbm = pl.BlockSpec(memory_space=pl.ANY)
    dma = pltpu.SemaphoreType.DMA
    bf16, f32 = jnp.bfloat16, jnp.float32
    out = pl.pallas_call(
        functools.partial(trak_kernel, nc, nf, positions, group, handed),
        out_shape=jax.ShapeDtypeStruct((images, kq, lanes), f32),
        in_specs=[hbm, hbm, hbm, vmem, hbm, vmem, hbm],
        out_specs=vmem,
        scratch_shapes=[
            pltpu.VMEM((nf, chunks, depth, cw), bf16),
            pltpu.VMEM((nc, rows, share), bf16),
            pltpu.VMEM((images, ka, positions), bf16),
            pltpu.VMEM((2, rows, cw), bf16),
            pltpu.VMEM((chunks, images, ka, cw), bf16),
            pltpu.VMEM((images, cw), f32),
            pltpu.VMEM((chunks, nf, images, cw), bf16),
            pltpu.VMEM((slots, cw, classes), bf16),
            pltpu.VMEM((nc, part, classes), f32),
            pltpu.VMEM((nc, part, classes), f32),
            pltpu.VMEM((nf, part, 128), f32),
            pltpu.VMEM((nc, part, classes), bf16 if part % 16 == 0 else f32),
            pltpu.VMEM((chunks, nf, images, cw), bf16),
            pltpu.VMEM((chunks, nf, images, cw), bf16),
            pltpu.VMEM((lanes, width), bf16),
            pltpu.VMEM((images * ka, lanes), f32),
            pltpu.VMEM((nc, images, kq, lanes), f32),
            pltpu.VMEM((nc, images, kq, lanes), f32),
            dma((chunks,)),
            dma((nf, chunks)),
            dma((nf, chunks)),
            dma((nf, chunks)),
            dma((nc,)),
            dma((nc,)),
            dma,
            dma((2,)),
            dma((nf, chunks)),
            dma((nf, chunks)),
            dma((slots,)),
            dma((nc,)),
            dma((nc,)),
            dma((nf,)),
            dma((nf,)),
            dma((nc,)),
            dma((nc,)),
            dma((nf, chunks)),
            dma((nf, chunks)),
            dma,
            dma((nc,)),
            dma((nc,)),
        ] + ([
            pltpu.VMEM((nc, rows, share), bf16),
            pltpu.VMEM((rows, handed * cw), bf16),
            pltpu.VMEM((images, ka, positions), bf16),
            pltpu.VMEM((handed, images, ka, cw), bf16),
            dma((chunks,)),
            dma((chunks,)),
            dma((chunks,)),
            dma((chunks,)),
            dma((nc, chunks)),
            dma((nc, chunks)),
            dma((nf, handed)),
            dma((handed,)),
            dma((handed,)),
        ] if handed else []),
        compiler_params=pltpu.CompilerParams(
            collective_id=0, has_side_effects=True, vmem_limit_bytes=62 * 2**20
        ),
        cost_estimate=pl.CostEstimate(
            flops=2 * rows * width * depth * nf + 4 * everyone * width * classes,
            bytes_accessed=2 * rows * width + 2 * depth * width + 4 * width * classes,
            transcendentals=part * classes,
        ),
    )(
        stream.reshape(rows, width), mid.reshape(rows, share), conv_weight, proj_act.T,
        head_weight, labels.reshape(nc, part, 1), proj_err.T,
    )
    return out[:, :, :ke].reshape(images, kq * ke)


def solution(mesh):
    in_specs = (
        P(("seed", "fsdp"), None, "chan"),
        P(("seed", "fsdp"), None, "chan"),
        P(("seed", "fsdp"), "chan"),
        P(("seed", "chan"), "fsdp"),
        P(),
        P(),
        P("chan", None),
    )
    out_specs = P(("seed", "fsdp"), "chan")
    return jax.shard_map(
        functools.partial(per_device, mesh.shape["chan"], mesh.shape["fsdp"]),
        mesh=mesh, in_specs=in_specs, out_specs=out_specs, check_vma=False,
    )
```

```python
import functools

import jax
import jax.numpy as jnp
from jax import lax
from jax.experimental import pallas as pl
from jax.experimental.pallas import tpu as pltpu
from jax.sharding import PartitionSpec as P

MESH = pl.DeviceIdType.MESH
AHEAD = 3


def trak_kernel(
    nc, nf, positions, group, handed,
    stream_ref, mid_ref, weight_ref, proj_ref, head_ref, labels_ref, perr_ref,
    out_ref,
    weights, mids, acts, held, cross, mean, pools, heads, logits, logits_in,
    totals, dlogits, dpool, dpool_in, perr, grads, shares, shares_in,
    own_sem, right_sem, left_sem, in_sem, mid_send, mid_recv, mid_own, held_sem,
    pool_send, pool_recv, head_sem, logit_send, logit_recv, total_send, total_recv,
    dlog_send, dlog_recv, dpool_send, dpool_recv, perr_sem, share_send, share_recv,
    *handed_refs,
):
    c = lax.axis_index("chan")
    f = lax.axis_index("fsdp")
    chunks, depth, cw = weights.shape[1:]
    share = mids.shape[2]
    rows = mids.shape[1]
    images = rows // positions
    full = chunks - handed
    inner = (f > 0) & (f < nf - 1)
    if handed:
        (
            mids_end, streams_end, acts_end, cross_end, piece_send, piece_recv, strip_send, strip_recv,
            pass_send, pass_recv, pool_end_send, cross_end_send, cross_end_recv,
        ) = handed_refs
        inward = jnp.where(f == 0, 1, nf - 2)
        end = jnp.where(f == 1, 0, nf - 1)

    def served(to, j):
        return ((to > 0) & (to < nf - 1)) | (j < full)

    def piece_rows(j):
        return pl.ds(pl.multiple_of(j * positions, 16), positions)

    def piece_copy(j):
        return pltpu.make_async_remote_copy(
            src_ref=mid_ref.at[piece_rows(j)], dst_ref=mids_end.at[c, piece_rows(j)],
            send_sem=piece_send.at[j], recv_sem=piece_recv.at[j],
            device_id={"fsdp": inward}, device_id_type=MESH,
        )

    def strip_copy(j):
        return pltpu.make_async_remote_copy(
            src_ref=stream_ref.at[piece_rows(j), full * cw :], dst_ref=streams_end.at[piece_rows(j)],
            send_sem=strip_send.at[j], recv_sem=strip_recv.at[j],
            device_id={"fsdp": inward}, device_id_type=MESH,
        )

    def pass_copy(j, d):
        return pltpu.make_async_remote_copy(
            src_ref=mids_end.at[c, piece_rows(j)], dst_ref=mids_end.at[c, piece_rows(j)],
            send_sem=pass_send.at[d, j], recv_sem=pass_recv.at[d, j],
            device_id={"chan": lax.rem(c + d, nc)}, device_id_type=MESH,
        )

    def cross_copy(k):
        return pltpu.make_async_remote_copy(
            src_ref=cross_end.at[k - full], dst_ref=cross.at[k],
            send_sem=cross_end_send.at[k - full], recv_sem=cross_end_recv.at[k - full],
            device_id={"fsdp": end}, device_id_type=MESH,
        )

    def own_copy(j):
        return pltpu.make_async_copy(
            weight_ref.at[:, pl.ds(pl.multiple_of(j * cw, cw), cw)], weights.at[f, j], own_sem.at[j]
        )

    def hop(b, j, right):
        return pltpu.make_async_remote_copy(
            src_ref=weights.at[b, j],
            dst_ref=weights.at[b, j],
            send_sem=(right_sem if right else left_sem).at[b, j],
            recv_sem=in_sem.at[b, j],
            device_id={"fsdp": f + 1 if right else f - 1},
            device_id_type=MESH,
        )

    def mid_copy(d):
        to = lax.rem(c + d, nc)
        return pltpu.make_async_remote_copy(
            src_ref=mid_ref,
            dst_ref=mids.at[c],
            send_sem=mid_send.at[d],
            recv_sem=mid_recv.at[d],
            device_id={"chan": to},
            device_id_type=MESH,
        )

    def stream_copy(k):
        slot = lax.rem(k, 2)
        return pltpu.make_async_copy(
            stream_ref.at[:, pl.ds(pl.multiple_of(k * cw, cw), cw)], held.at[slot], held_sem.at[slot]
        )

    lax.fori_loop(0, chunks, lambda j, x: (own_copy(j).start(), x)[1], 0)
    own_mid = pltpu.make_async_copy(mid_ref, mids.at[c], mid_own)
    own_mid.start()
    stream_copy(0).start()

    classes = head_ref.shape[1]
    tile = min(1024, classes)
    slots = heads.shape[0]
    part = logits.shape[1]

    def head_copy(t):
        slot = lax.rem(t, slots)
        return pltpu.make_async_copy(
            head_ref.at[pl.ds(pl.multiple_of(lax.rem(t, chunks) * cw, cw), cw), :],
            heads.at[slot], head_sem.at[slot],
        )

    def to_chan(src, dst, send, recv, d):
        return pltpu.make_async_remote_copy(
            src_ref=src, dst_ref=dst, send_sem=send.at[d], recv_sem=recv.at[d],
            device_id={"chan": lax.rem(c + d, nc)}, device_id_type=MESH,
        )

    def to_fsdp(src, dst, send, recv, d):
        return pltpu.make_async_remote_copy(
            src_ref=src, dst_ref=dst, send_sem=send, recv_sem=recv,
            device_id={"fsdp": lax.rem(f + d, nf)}, device_id_type=MESH,
        )

    def pool_copy(k, d):
        return to_fsdp(pools.at[k, f], pools.at[k, f], pool_send.at[d, k], pool_recv.at[f, k], d)

    def pool_end_copy(k, d):
        return to_fsdp(
            pools.at[k, end], pools.at[k, end], pool_end_send.at[d, k - full], pool_recv.at[end, k], d
        )

    def pool_arrival(k, b):
        return to_fsdp(pools.at[k, b], pools.at[k, b], pool_send.at[1, k], pool_recv.at[b, k], 1)

    def logit_copy(d, g):
        span = pl.ds(pl.multiple_of(g * tile, tile), tile)
        return to_chan(
            logits.at[lax.rem(c + d, nc), :, span], logits_in.at[c, :, span], logit_send.at[g], logit_recv.at[g], d
        )

    def total_copy(d):
        return to_fsdp(totals.at[f], totals.at[f], total_send.at[d], total_recv.at[d], d)

    def dlog_copy(d, g):
        span = pl.ds(pl.multiple_of(g * tile, tile), tile)
        return to_chan(dlogits.at[c, :, span], dlogits.at[c, :, span], dlog_send.at[g], dlog_recv.at[g], d)

    def dpool_copy(k, d):
        return to_fsdp(
            dpool.at[k, lax.rem(f + d, nf)], dpool_in.at[k, f], dpool_send.at[d, k], dpool_recv.at[d, k], d
        )

    def share_copy(d):
        return to_chan(shares.at[lax.rem(c + d, nc)], shares_in.at[c], share_send, share_recv, d)

    for t in range(slots):
        head_copy(t).start()
    perr_copy = pltpu.make_async_copy(perr_ref, perr.at[0 : perr_ref.shape[0]], perr_sem)
    perr_copy.start()
    perr[perr_ref.shape[0] :] = jnp.zeros(
        (perr.shape[0] - perr_ref.shape[0], perr.shape[1]), perr.dtype
    )
    logits[...] = jnp.zeros_like(logits)

    barrier = pltpu.get_barrier_semaphore()
    for d in range(1, nc):
        pl.semaphore_signal(barrier, 1, device_id={"chan": lax.rem(c + d, nc)}, device_id_type=MESH)

    for d in range(1, nf):
        pl.semaphore_signal(barrier, 1, device_id={"fsdp": lax.rem(f + d, nf)}, device_id_type=MESH)
    pl.semaphore_wait(barrier, nc - 1 + nf - 1)

    for d in range(1, nc):
        mid_copy(d).start()

    def send_own(j):
        own_copy(j).wait()

        @pl.when((f < nf - 1) & served(f + 1, j))
        def _():
            hop(f, j, True).start()

        @pl.when((f > 0) & served(f - 1, j))
        def _():
            hop(f, j, False).start()

        if handed:
            @pl.when(jnp.logical_not(inner))
            def _():
                piece_copy(j).start()
                strip_copy(j).start()

    for j in range(min(AHEAD, chunks)):
        send_own(j)

    def relay(r):
        @pl.when(r + AHEAD < chunks)
        def _():
            send_own(r + AHEAD)

        for d in range(1, nf):
            @pl.when((f - d >= 0) & served(f, r))
            def _():
                hop(f - d, r, True).wait_recv()

                @pl.when((f < nf - 1) & served(f + 1, r))
                def _():
                    hop(f - d, r, True).start()

            @pl.when((f + d < nf) & served(f, r))
            def _():
                hop(f + d, r, False).wait_recv()

                @pl.when((f > 0) & served(f - 1, r))
                def _():
                    hop(f + d, r, False).start()

        if handed:
            @pl.when(inner & (r >= chunks // 2))
            def _():
                for q in range(2):
                    j = 2 * (r - chunks // 2) + q
                    piece_copy(j).wait_recv()
                    for d in range(1, nc):
                        pass_copy(j, d).start()

    step = min(depth, share)
    pieces = nf * depth // step

    def compute(k):
        stream_copy(k).wait()

        @pl.when((k + 1 < chunks) & served(f, k + 1))
        def _():
            stream_copy(k + 1).start()

        slot = lax.rem(k, 2)
        convolve(k, mids, acts, lambda span: held[slot, span, :], cross.at[k])
        pools[k, f] = mean[...].astype(jnp.bfloat16)
        for d in range(1, nf):
            pool_copy(k, d).start()

    def compute_end(k):
        at = (k - full) * cw
        convolve(k, mids_end, acts_end, lambda span: streams_end[span, at : at + cw], cross_end.at[k - full])
        pools[k, end] = mean[...].astype(jnp.bfloat16)
        for d in range(1, nf):
            pool_end_copy(k, d).start()
        cross_copy(k).start()

    def convolve(k, mids, acts, load, sums):
        def some(g, x):
            span = pl.ds(pl.multiple_of(g * group * positions, 16), group * positions)
            y = load(span).astype(jnp.float32)
            for s in range(pieces):
                at = s * step
                y += jnp.dot(
                    mids[at // share, span, at % share : at % share + step],
                    weights[at // depth, k, at % depth : at % depth + step, :],
                    preferred_element_type=jnp.float32,
                )
            for i in range(group):
                one = y[i * positions : (i + 1) * positions]
                total = jnp.sum(jnp.maximum(one, 0.0), axis=0, keepdims=True)
                mean[pl.ds(g * group + i, 1), :] = total / positions
                mask = jnp.where(one > 0.0, 1.0, 0.0).astype(jnp.bfloat16)
                sums[g * group + i] = jnp.dot(
                    acts[g * group + i], mask, preferred_element_type=jnp.float32
                ).astype(sums.dtype)
            return x

        lax.fori_loop(0, images // group, some, 0)

    def add_logits(k, late=False, final=False):
        head_copy(k).wait()
        for b in range(nf):
            here = f == b
            if late:
                here = inner & (here | (end == b))

            @pl.when(jnp.logical_not(here))
            def _():
                pool_arrival(k, b).wait_recv()

        slot = lax.rem(k, slots)
        rows_all = pools[k].reshape(nf * images, cw)

        def some(g, x):
            span = pl.ds(pl.multiple_of(g * tile, tile), tile)
            add = jnp.dot(rows_all, heads[slot, :, span], preferred_element_type=jnp.float32)
            for q in range(nc):
                logits[q, :, span] += add[q * part : (q + 1) * part]
            if final:
                for d in range(1, nc):
                    logit_copy(d, g).start()
            return x

        lax.fori_loop(0, classes // tile, some, 0)
        head_copy(k + slots).start()

    def project(mids, acts):
        def one(i, x):
            span = pl.ds(pl.multiple_of(i * positions, 16), positions)
            out = jnp.zeros((proj_ref.shape[0], positions), jnp.float32)
            for q in range(nc):
                out += lax.dot_general(
                    proj_ref[:, q * share : (q + 1) * share], mids[q, span, :],
                    (((1,), (1,)), ((), ())), preferred_element_type=jnp.float32,
                )
            acts[i] = out.astype(jnp.bfloat16)
            return x

        lax.fori_loop(0, images, one, 0)

    last = max(full - 2, 0) // 2 * 2
    first = last // 2
    lax.fori_loop(0, first, lambda r, x: (relay(r), x)[1], 0)
    own_mid.wait()
    for d in range(1, nc):
        mid_copy(d).wait_recv()
    project(mids, acts)

    def pair(r, x):
        relay(r)
        compute(2 * (r - first))
        compute(2 * (r - first) + 1)

        @pl.when(r > first)
        def _():
            add_logits(2 * (r - first) - 2)
            add_logits(2 * (r - first) - 1)

        return x

    lax.fori_loop(first, last, pair, 0)

    def single(r, x):
        relay(r)
        compute(r)

        @pl.when(r >= 2)
        def _():
            add_logits(r - 2)

        return x

    lax.fori_loop(last, full, single, 0)
    if handed:
        @pl.when(inner)
        def _():
            for r in range(full, chunks):
                relay(r)
                compute(r)

            def arrived(j, x):
                strip_copy(j).wait_recv()
                for d in range(1, nc):
                    pass_copy(j, d).wait_recv()
                return x

            lax.fori_loop(0, images, arrived, 0)
            project(mids_end, acts_end)
            for k in range(full, chunks):
                compute_end(k)

    for k in range(max(full - 2, 0), chunks):
        add_logits(k, k >= full, k == chunks - 1)

    def drain(j, x):
        @pl.when((f < nf - 1) & served(f + 1, j))
        def _():
            for d in range(nf):
                @pl.when(f - d >= 0)
                def _():
                    hop(f - d, j, True).wait_send()

        @pl.when((f > 0) & served(f - 1, j))
        def _():
            for d in range(nf):
                @pl.when(f + d < nf)
                def _():
                    hop(f + d, j, False).wait_send()

        @pl.when(served(f, j))
        def _():
            for d in range(1, nf):
                pool_copy(j, d).wait_send()

        if handed:
            @pl.when(jnp.logical_not(inner))
            def _():
                piece_copy(j).wait_send()
                strip_copy(j).wait_send()

            @pl.when(inner)
            def _():
                for d in range(1, nc):
                    pass_copy(j, d).wait_send()

        return x

    lax.fori_loop(0, chunks, drain, 0)
    for d in range(1, nc):
        mid_copy(d).wait_send()

    def exponents(g, total):
        for d in range(1, nc):
            logit_copy(d, g).wait_recv()
        span = pl.ds(pl.multiple_of(g * tile, tile), tile)
        value = logits[c, :, span]
        for d in range(1, nc):
            value += logits_in[lax.rem(c + nc - d, nc), :, span]
        value = jnp.exp(value)
        logits[c, :, span] = value
        return total + jnp.sum(value, axis=1, keepdims=True)

    total = lax.fori_loop(0, classes // tile, exponents, jnp.zeros((part, 1), jnp.float32))
    totals[f] = jnp.broadcast_to(total, totals.shape[1:])
    for d in range(1, nf):
        total_copy(d).start()
    for d in range(1, nf):
        total_copy(d).wait_recv()
    total = jnp.sum(totals[...], axis=0)[:, :1]

    def derivatives(g, x):
        span = pl.ds(pl.multiple_of(g * tile, tile), tile)
        ids = f * classes + g * tile + lax.broadcasted_iota(jnp.int32, (part, tile), 1)
        onehot = jnp.where(labels_ref[c] == ids, 1.0, 0.0)
        dlogits[c, :, span] = (logits[c, :, span] / total - onehot).astype(dlogits.dtype)
        for d in range(1, nc):
            dlog_copy(d, g).start()
        return x

    lax.fori_loop(0, classes // tile, derivatives, 0)
    for g in range(classes // tile):
        for d in range(1, nc):
            dlog_copy(d, g).wait_recv()
    perr_copy.wait()
    grads[...] = jnp.zeros_like(grads)
    if handed:
        @pl.when(jnp.logical_not(inner))
        def _():
            for k in range(full, chunks):
                cross_copy(k).wait_recv()


    def back(k, x):
        head_copy(k + chunks).wait()
        if x is not None:
            arrivals(k - lag)
        slot = lax.rem(k + chunks, slots)
        grad = lax.dot_general(
            dlogits[...].reshape(nc * part, classes).astype(jnp.bfloat16), heads[slot],
            (((1,), (1,)), ((), ())), preferred_element_type=jnp.float32,
        )
        if x is not None:
            finish(k - lag)
        dpool[k] = grad.reshape(nf, images, cw).astype(jnp.bfloat16)
        for d in range(1, nf):
            dpool_copy(k, d).start()

        @pl.when(k + slots < chunks)
        def _():
            head_copy(k + chunks + slots).start()

        return x

    lag = min(4, chunks)

    def arrivals(k):
        for d in range(1, nf):
            dpool_copy(k, d).wait_recv()

    def finish(k):
        error = dpool[k, f].astype(jnp.float32)
        for d in range(1, nf):
            error += dpool_in[k, lax.rem(f + nf - d, nf)].astype(jnp.float32)
        error = (error / positions).astype(jnp.bfloat16).astype(jnp.float32)
        scaled = jnp.concatenate(
            [
                (cross[k, i].astype(jnp.float32) * error[i : i + 1]).astype(jnp.bfloat16)
                for i in range(images)
            ],
            axis=0,
        )
        grads[...] += lax.dot_general(
            scaled, perr[:, pl.ds(pl.multiple_of(k * cw, cw), cw)],
            (((1,), (1,)), ((), ())), preferred_element_type=jnp.float32,
        )

    for k in range(lag):
        back(k, None)
    lax.fori_loop(lag, chunks, back, 0)
    for k in range(chunks - lag, chunks):
        arrivals(k)
        finish(k)
    ka = proj_ref.shape[0]
    kq = ka // nc
    for q in range(nc):
        for i in range(images):
            shares[q, i] = grads[i * ka + q * kq : i * ka + (q + 1) * kq]
    for d in range(1, nc):
        share_copy(d).start()
    for d in range(1, nc):
        share_copy(d).wait_recv()
    result = shares[c]
    for d in range(1, nc):
        result += shares_in[lax.rem(c + nc - d, nc)]
    out_ref[...] = result

    if handed:
        @pl.when(inner)
        def _():
            for k in range(full, chunks):
                cross_copy(k).wait_send()
                for d in range(1, nf):
                    pool_end_copy(k, d).wait_send()

    def drain_late(j, x):
        for d in range(1, nf):
            dpool_copy(j, d).wait_send()
        return x

    lax.fori_loop(0, chunks, drain_late, 0)
    for d in range(1, nc):
        for g in range(classes // tile):
            logit_copy(d, g).wait_send()
            dlog_copy(d, g).wait_send()
        share_copy(d).wait_send()
    for d in range(1, nf):
        total_copy(d).wait_send()


def per_device(nc, nf, stream, mid, conv_weight, head_weight, labels, proj_act, proj_err):
    images, positions, width = stream.shape
    rows = images * positions
    share = mid.shape[2]
    depth = conv_weight.shape[0]
    ka, ke = proj_act.shape[1], proj_err.shape[1]
    classes = head_weight.shape[1]
    everyone = images * nf
    part = everyone // nc
    kq = ka // nc
    lanes = max(ke, 128)
    cw = min(256, width)
    chunks = width // cw
    slots = min(8, chunks)
    handed = 0
    group = 4
    vmem = pl.BlockSpec(memory_space=pltpu.VMEM)
    hbm = pl.BlockSpec(memory_space=pl.ANY)
    dma = pltpu.SemaphoreType.DMA
    bf16, f32 = jnp.bfloat16, jnp.float32
    out = pl.pallas_call(
        functools.partial(trak_kernel, nc, nf, positions, group, handed),
        out_shape=jax.ShapeDtypeStruct((images, kq, lanes), f32),
        in_specs=[hbm, hbm, hbm, vmem, hbm, vmem, hbm],
        out_specs=vmem,
        scratch_shapes=[
            pltpu.VMEM((nf, chunks, depth, cw), bf16),
            pltpu.VMEM((nc, rows, share), bf16),
            pltpu.VMEM((images, ka, positions), bf16),
            pltpu.VMEM((2, rows, cw), bf16),
            pltpu.VMEM((chunks, images, ka, cw), bf16),
            pltpu.VMEM((images, cw), f32),
            pltpu.VMEM((chunks, nf, images, cw), bf16),
            pltpu.VMEM((slots, cw, classes), bf16),
            pltpu.VMEM((nc, part, classes), f32),
            pltpu.VMEM((nc, part, classes), f32),
            pltpu.VMEM((nf, part, 128), f32),
            pltpu.VMEM((nc, part, classes), bf16 if part % 16 == 0 else f32),
            pltpu.VMEM((chunks, nf, images, cw), bf16),
            pltpu.VMEM((chunks, nf, images, cw), bf16),
            pltpu.VMEM((lanes, width), bf16),
            pltpu.VMEM((images * ka, lanes), f32),
            pltpu.VMEM((nc, images, kq, lanes), f32),
            pltpu.VMEM((nc, images, kq, lanes), f32),
            dma((chunks,)),
            dma((nf, chunks)),
            dma((nf, chunks)),
            dma((nf, chunks)),
            dma((nc,)),
            dma((nc,)),
            dma,
            dma((2,)),
            dma((nf, chunks)),
            dma((nf, chunks)),
            dma((slots,)),
            dma((classes // min(1024, classes), nc)),
            dma((classes // min(1024, classes), nc)),
            dma((nf,)),
            dma((nf,)),
            dma((classes // min(1024, classes), nc)),
            dma((classes // min(1024, classes), nc)),
            dma((nf, chunks)),
            dma((nf, chunks)),
            dma,
            dma((nc,)),
            dma((nc,)),
        ] + ([
            pltpu.VMEM((nc, rows, share), bf16),
            pltpu.VMEM((rows, handed * cw), bf16),
            pltpu.VMEM((images, ka, positions), bf16),
            pltpu.VMEM((handed, images, ka, cw), bf16),
            dma((chunks,)),
            dma((chunks,)),
            dma((chunks,)),
            dma((chunks,)),
            dma((nc, chunks)),
            dma((nc, chunks)),
            dma((nf, handed)),
            dma((handed,)),
            dma((handed,)),
        ] if handed else []),
        compiler_params=pltpu.CompilerParams(
            collective_id=0, has_side_effects=True, vmem_limit_bytes=62 * 2**20
        ),
        cost_estimate=pl.CostEstimate(
            flops=2 * rows * width * depth * nf + 4 * everyone * width * classes,
            bytes_accessed=2 * rows * width + 2 * depth * width + 4 * width * classes,
            transcendentals=part * classes,
        ),
    )(
        stream.reshape(rows, width), mid.reshape(rows, share), conv_weight, proj_act.T,
        head_weight, labels.reshape(nc, part, 1), proj_err.T,
    )
    return out[:, :, :ke].reshape(images, kq * ke)


def solution(mesh):
    in_specs = (
        P(("seed", "fsdp"), None, "chan"),
        P(("seed", "fsdp"), None, "chan"),
        P(("seed", "fsdp"), "chan"),
        P(("seed", "chan"), "fsdp"),
        P(),
        P(),
        P("chan", None),
    )
    out_specs = P(("seed", "fsdp"), "chan")
    return jax.shard_map(
        functools.partial(per_device, mesh.shape["chan"], mesh.shape["fsdp"]),
        mesh=mesh, in_specs=in_specs, out_specs=out_specs, check_vma=False,
    )
```

```python
import functools

import jax
import jax.numpy as jnp
from jax import lax
from jax.experimental import pallas as pl
from jax.experimental.pallas import tpu as pltpu
from jax.sharding import PartitionSpec as P

MESH = pl.DeviceIdType.MESH
AHEAD = 3


def trak_kernel(
    nc, nf, positions, group,
    stream_ref, mid_ref, weight_ref, proj_ref, head_ref, labels_ref, perr_ref,
    out_ref,
    weights, mids, acts, held, cross, mean, pools, heads, logits, logits_in,
    totals, dlogits, dpool, dpool_in, perr, grads, shares, shares_in,
    own_sem, right_sem, left_sem, in_sem, mid_send, mid_recv, mid_own, held_sem,
    pool_send, pool_recv, head_sem, logit_send, logit_recv, total_send, total_recv,
    dlog_send, dlog_recv, dpool_send, dpool_recv, perr_sem, share_send, share_recv,
):
    c = lax.axis_index("chan")
    f = lax.axis_index("fsdp")
    chunks, depth, cw = weights.shape[1:]
    share = mids.shape[2]
    rows = mids.shape[1]
    images = rows // positions

    def own_copy(j):
        return pltpu.make_async_copy(
            weight_ref.at[:, pl.ds(pl.multiple_of(j * cw, cw), cw)], weights.at[f, j], own_sem.at[j]
        )

    def hop(b, j, right):
        return pltpu.make_async_remote_copy(
            src_ref=weights.at[b, j],
            dst_ref=weights.at[b, j],
            send_sem=(right_sem if right else left_sem).at[b, j],
            recv_sem=in_sem.at[b, j],
            device_id={"fsdp": f + 1 if right else f - 1},
            device_id_type=MESH,
        )

    def mid_copy(d):
        to = lax.rem(c + d, nc)
        return pltpu.make_async_remote_copy(
            src_ref=mid_ref,
            dst_ref=mids.at[c],
            send_sem=mid_send.at[d],
            recv_sem=mid_recv.at[d],
            device_id={"chan": to},
            device_id_type=MESH,
        )

    def stream_copy(k):
        slot = lax.rem(k, 2)
        return pltpu.make_async_copy(
            stream_ref.at[:, pl.ds(pl.multiple_of(k * cw, cw), cw)], held.at[slot], held_sem.at[slot]
        )

    lax.fori_loop(0, chunks, lambda j, x: (own_copy(j).start(), x)[1], 0)
    own_mid = pltpu.make_async_copy(mid_ref, mids.at[c], mid_own)
    own_mid.start()
    stream_copy(0).start()

    classes = head_ref.shape[1]
    tile = min(1024, classes)
    slots = heads.shape[0]
    part = logits.shape[1]

    def head_copy(t):
        slot = lax.rem(t, slots)
        return pltpu.make_async_copy(
            head_ref.at[pl.ds(pl.multiple_of(lax.rem(t, chunks) * cw, cw), cw), :],
            heads.at[slot], head_sem.at[slot],
        )

    def to_chan(src, dst, send, recv, d):
        return pltpu.make_async_remote_copy(
            src_ref=src, dst_ref=dst, send_sem=send.at[d], recv_sem=recv.at[d],
            device_id={"chan": lax.rem(c + d, nc)}, device_id_type=MESH,
        )

    def to_fsdp(src, dst, send, recv, d):
        return pltpu.make_async_remote_copy(
            src_ref=src, dst_ref=dst, send_sem=send, recv_sem=recv,
            device_id={"fsdp": lax.rem(f + d, nf)}, device_id_type=MESH,
        )

    def pool_copy(k, d):
        return to_fsdp(pools.at[k, f], pools.at[k, f], pool_send.at[d, k], pool_recv.at[d, k], d)

    def logit_copy(d):
        return to_chan(logits.at[lax.rem(c + d, nc)], logits_in.at[c], logit_send, logit_recv, d)

    def total_copy(d):
        return to_fsdp(totals.at[f], totals.at[f], total_send.at[d], total_recv.at[d], d)

    def dlog_copy(d):
        return to_chan(dlogits.at[c], dlogits.at[c], dlog_send, dlog_recv, d)

    def dpool_copy(k, d):
        return to_fsdp(
            dpool.at[k, lax.rem(f + d, nf)], dpool_in.at[k, f], dpool_send.at[d, k], dpool_recv.at[d, k], d
        )

    def share_copy(d):
        return to_chan(shares.at[lax.rem(c + d, nc)], shares_in.at[c], share_send, share_recv, d)

    for t in range(slots):
        head_copy(t).start()
    perr_copy = pltpu.make_async_copy(perr_ref, perr.at[0 : perr_ref.shape[0]], perr_sem)
    perr_copy.start()
    perr[perr_ref.shape[0] :] = jnp.zeros(
        (perr.shape[0] - perr_ref.shape[0], perr.shape[1]), perr.dtype
    )
    logits[...] = jnp.zeros_like(logits)

    barrier = pltpu.get_barrier_semaphore()
    for d in range(1, nc):
        pl.semaphore_signal(barrier, 1, device_id={"chan": lax.rem(c + d, nc)}, device_id_type=MESH)

    for d in range(1, nf):
        pl.semaphore_signal(barrier, 1, device_id={"fsdp": lax.rem(f + d, nf)}, device_id_type=MESH)
    pl.semaphore_wait(barrier, nc - 1 + nf - 1)

    for d in range(1, nc):
        mid_copy(d).start()

    def send_own(j):
        own_copy(j).wait()

        @pl.when(f < nf - 1)
        def _():
            hop(f, j, True).start()

        @pl.when(f > 0)
        def _():
            hop(f, j, False).start()

    for j in range(min(AHEAD, chunks)):
        send_own(j)

    def relay(r):
        @pl.when(r + AHEAD < chunks)
        def _():
            send_own(r + AHEAD)

        for d in range(1, nf):
            @pl.when(f - d >= 0)
            def _():
                hop(f - d, r, True).wait_recv()

                @pl.when(f < nf - 1)
                def _():
                    hop(f - d, r, True).start()

            @pl.when(f + d < nf)
            def _():
                hop(f + d, r, False).wait_recv()

                @pl.when(f > 0)
                def _():
                    hop(f + d, r, False).start()

    step = min(depth, share)
    pieces = nf * depth // step

    def compute(k):
        stream_copy(k).wait()

        @pl.when(k + 1 < chunks)
        def _():
            stream_copy(k + 1).start()

        slot = lax.rem(k, 2)

        def some(g, x):
            span = pl.ds(pl.multiple_of(g * group * positions, 16), group * positions)
            y = held[slot, span, :].astype(jnp.float32)
            for s in range(pieces):
                at = s * step
                y += jnp.dot(
                    mids[at // share, span, at % share : at % share + step],
                    weights[at // depth, k, at % depth : at % depth + step, :],
                    preferred_element_type=jnp.float32,
                )
            for i in range(group):
                one = y[i * positions : (i + 1) * positions]
                total = jnp.sum(jnp.maximum(one, 0.0), axis=0, keepdims=True)
                mean[pl.ds(g * group + i, 1), :] = total / positions
                mask = jnp.where(one > 0.0, 1.0, 0.0).astype(jnp.bfloat16)
                cross[k, g * group + i] = jnp.dot(
                    acts[g * group + i], mask, preferred_element_type=jnp.float32
                ).astype(cross.dtype)
            return x

        lax.fori_loop(0, images // group, some, 0)
        pools[k, f] = mean[...].astype(jnp.bfloat16)
        for d in range(1, nf):
            pool_copy(k, d).start()

    def add_logits(k):
        head_copy(k).wait()
        for d in range(1, nf):
            pool_copy(k, d).wait_recv()
        slot = lax.rem(k, slots)
        rows_all = pools[k].reshape(nf * images, cw)

        def some(g, x):
            span = pl.ds(pl.multiple_of(g * tile, tile), tile)
            add = jnp.dot(rows_all, heads[slot, :, span], preferred_element_type=jnp.float32)
            for q in range(nc):
                logits[q, :, span] += add[q * part : (q + 1) * part]
            return x

        lax.fori_loop(0, classes // tile, some, 0)
        head_copy(k + slots).start()

    def project():
        own_mid.wait()
        for d in range(1, nc):
            mid_copy(d).wait_recv()

        def one(i, x):
            span = pl.ds(pl.multiple_of(i * positions, 16), positions)
            out = jnp.zeros((proj_ref.shape[0], positions), jnp.float32)
            for q in range(nc):
                out += lax.dot_general(
                    proj_ref[:, q * share : (q + 1) * share], mids[q, span, :],
                    (((1,), (1,)), ((), ())), preferred_element_type=jnp.float32,
                )
            acts[i] = out.astype(jnp.bfloat16)
            return x

        lax.fori_loop(0, images, one, 0)

    end = (f == 0) | (f == nf - 1)
    first = max(chunks // 2 - 1, 0)
    last = max(chunks - 2, 0)
    lax.fori_loop(0, first, lambda r, x: (relay(r), x)[1], 0)
    project()

    def pair(r, x):
        relay(r)
        compute(2 * (r - first))
        compute(2 * (r - first) + 1)

        @pl.when(end & (r > first))
        def _():
            add_logits(2 * (r - first) - 2)
            add_logits(2 * (r - first) - 1)

        @pl.when(jnp.logical_not(end) & (r > first + 1))
        def _():
            add_logits(2 * (r - first) - 4)
            add_logits(2 * (r - first) - 3)

        return x

    lax.fori_loop(first, last, pair, 0)

    def single(r, x):
        relay(r)
        compute(r)

        @pl.when(end & (r >= 2))
        def _():
            add_logits(r - 2)

        return x

    lax.fori_loop(last, chunks, single, 0)

    @pl.when(jnp.logical_not(end))
    def _():
        lax.fori_loop(max(last - 4, 0), last, lambda k, x: (add_logits(k), x)[1], 0)

    for k in range(last, chunks):
        add_logits(k)

    for d in range(1, nc):
        logit_copy(d).start()
    for d in range(1, nc):
        logit_copy(d).wait_recv()

    def exponents(g, total):
        span = pl.ds(pl.multiple_of(g * tile, tile), tile)
        value = logits[c, :, span]
        for d in range(1, nc):
            value += logits_in[lax.rem(c + nc - d, nc), :, span]
        value = jnp.exp(value)
        logits[c, :, span] = value
        return total + jnp.sum(value, axis=1, keepdims=True)

    total = lax.fori_loop(0, classes // tile, exponents, jnp.zeros((part, 1), jnp.float32))
    totals[f] = jnp.broadcast_to(total, totals.shape[1:])
    for d in range(1, nf):
        total_copy(d).start()
    for d in range(1, nf):
        total_copy(d).wait_recv()
    total = jnp.sum(totals[...], axis=0)[:, :1]

    def derivatives(g, x):
        span = pl.ds(pl.multiple_of(g * tile, tile), tile)
        ids = f * classes + g * tile + lax.broadcasted_iota(jnp.int32, (part, tile), 1)
        onehot = jnp.where(labels_ref[c] == ids, 1.0, 0.0)
        dlogits[c, :, span] = (logits[c, :, span] / total - onehot).astype(dlogits.dtype)
        return x

    lax.fori_loop(0, classes // tile, derivatives, 0)
    for d in range(1, nc):
        dlog_copy(d).start()
    for d in range(1, nc):
        dlog_copy(d).wait_recv()

    def back(k, x):
        head_copy(k + chunks).wait()
        slot = lax.rem(k + chunks, slots)
        grad = lax.dot_general(
            dlogits[...].reshape(nc * part, classes).astype(jnp.bfloat16), heads[slot],
            (((1,), (1,)), ((), ())), preferred_element_type=jnp.float32,
        )
        dpool[k] = grad.reshape(nf, images, cw).astype(jnp.bfloat16)
        for d in range(1, nf):
            dpool_copy(k, d).start()

        @pl.when(k + slots < chunks)
        def _():
            head_copy(k + chunks + slots).start()

        return x

    lax.fori_loop(0, chunks, back, 0)
    perr_copy.wait()
    grads[...] = jnp.zeros_like(grads)

    def finish(k, x):
        error = dpool[k, f].astype(jnp.float32)
        for d in range(1, nf):
            dpool_copy(k, d).wait_recv()
        for d in range(1, nf):
            error += dpool_in[k, lax.rem(f + nf - d, nf)].astype(jnp.float32)
        error = (error / positions).astype(jnp.bfloat16).astype(jnp.float32)
        scaled = jnp.concatenate(
            [
                (cross[k, i].astype(jnp.float32) * error[i : i + 1]).astype(jnp.bfloat16)
                for i in range(images)
            ],
            axis=0,
        )
        grads[...] += lax.dot_general(
            scaled, perr[:, pl.ds(pl.multiple_of(k * cw, cw), cw)],
            (((1,), (1,)), ((), ())), preferred_element_type=jnp.float32,
        )
        return x

    lax.fori_loop(0, chunks, finish, 0)
    ka = proj_ref.shape[0]
    kq = ka // nc
    for q in range(nc):
        for i in range(images):
            shares[q, i] = grads[i * ka + q * kq : i * ka + (q + 1) * kq]
    for d in range(1, nc):
        share_copy(d).start()
    for d in range(1, nc):
        share_copy(d).wait_recv()
    result = shares[c]
    for d in range(1, nc):
        result += shares_in[lax.rem(c + nc - d, nc)]
    out_ref[...] = result

    def drain(j, x):
        @pl.when(f < nf - 1)
        def _():
            hop(f, j, True).wait_send()

        @pl.when(f > 0)
        def _():
            hop(f, j, False).wait_send()

        for d in range(1, nf):
            pool_copy(j, d).wait_send()
            dpool_copy(j, d).wait_send()

            @pl.when((f - d >= 0) & (f < nf - 1))
            def _():
                hop(f - d, j, True).wait_send()

            @pl.when((f + d < nf) & (f > 0))
            def _():
                hop(f + d, j, False).wait_send()

        return x

    lax.fori_loop(0, chunks, drain, 0)
    for d in range(1, nc):
        mid_copy(d).wait_send()
        logit_copy(d).wait_send()
        dlog_copy(d).wait_send()
        share_copy(d).wait_send()
    for d in range(1, nf):
        total_copy(d).wait_send()


def per_device(nc, nf, stream, mid, conv_weight, head_weight, labels, proj_act, proj_err):
    images, positions, width = stream.shape
    rows = images * positions
    share = mid.shape[2]
    depth = conv_weight.shape[0]
    ka, ke = proj_act.shape[1], proj_err.shape[1]
    classes = head_weight.shape[1]
    everyone = images * nf
    part = everyone // nc
    kq = ka // nc
    lanes = max(ke, 128)
    cw = min(256, width)
    chunks = width // cw
    slots = min(8, chunks)
    group = 4
    vmem = pl.BlockSpec(memory_space=pltpu.VMEM)
    hbm = pl.BlockSpec(memory_space=pl.ANY)
    dma = pltpu.SemaphoreType.DMA
    bf16, f32 = jnp.bfloat16, jnp.float32
    out = pl.pallas_call(
        functools.partial(trak_kernel, nc, nf, positions, group),
        out_shape=jax.ShapeDtypeStruct((images, kq, lanes), f32),
        in_specs=[hbm, hbm, hbm, vmem, hbm, vmem, hbm],
        out_specs=vmem,
        scratch_shapes=[
            pltpu.VMEM((nf, chunks, depth, cw), bf16),
            pltpu.VMEM((nc, rows, share), bf16),
            pltpu.VMEM((images, ka, positions), bf16),
            pltpu.VMEM((2, rows, cw), bf16),
            pltpu.VMEM((chunks, images, ka, cw), bf16),
            pltpu.VMEM((images, cw), f32),
            pltpu.VMEM((chunks, nf, images, cw), bf16),
            pltpu.VMEM((slots, cw, classes), bf16),
            pltpu.VMEM((nc, part, classes), f32),
            pltpu.VMEM((nc, part, classes), f32),
            pltpu.VMEM((nf, part, 128), f32),
            pltpu.VMEM((nc, part, classes), bf16 if part % 16 == 0 else f32),
            pltpu.VMEM((chunks, nf, images, cw), bf16),
            pltpu.VMEM((chunks, nf, images, cw), bf16),
            pltpu.VMEM((lanes, width), bf16),
            pltpu.VMEM((images * ka, lanes), f32),
            pltpu.VMEM((nc, images, kq, lanes), f32),
            pltpu.VMEM((nc, images, kq, lanes), f32),
            dma((chunks,)),
            dma((nf, chunks)),
            dma((nf, chunks)),
            dma((nf, chunks)),
            dma((nc,)),
            dma((nc,)),
            dma,
            dma((2,)),
            dma((nf, chunks)),
            dma((nf, chunks)),
            dma((slots,)),
            dma((nc,)),
            dma((nc,)),
            dma((nf,)),
            dma((nf,)),
            dma((nc,)),
            dma((nc,)),
            dma((nf, chunks)),
            dma((nf, chunks)),
            dma,
            dma((nc,)),
            dma((nc,)),
        ],
        compiler_params=pltpu.CompilerParams(
            collective_id=0, has_side_effects=True, vmem_limit_bytes=62 * 2**20
        ),
        cost_estimate=pl.CostEstimate(
            flops=2 * rows * width * depth * nf + 4 * everyone * width * classes,
            bytes_accessed=2 * rows * width + 2 * depth * width + 4 * width * classes,
            transcendentals=part * classes,
        ),
    )(
        stream.reshape(rows, width), mid.reshape(rows, share), conv_weight, proj_act.T,
        head_weight, labels.reshape(nc, part, 1), proj_err.T,
    )
    return out[:, :, :ke].reshape(images, kq * ke)


def solution(mesh):
    in_specs = (
        P(("seed", "fsdp"), None, "chan"),
        P(("seed", "fsdp"), None, "chan"),
        P(("seed", "fsdp"), "chan"),
        P(("seed", "chan"), "fsdp"),
        P(),
        P(),
        P("chan", None),
    )
    out_specs = P(("seed", "fsdp"), "chan")
    return jax.shard_map(
        functools.partial(per_device, mesh.shape["chan"], mesh.shape["fsdp"]),
        mesh=mesh, in_specs=in_specs, out_specs=out_specs, check_vma=False,
    )
```
